256 devices in a mesh: section: 4 (over y_hi, core), expert: 64 (over z, y_lo, x).
Axes of the slice: x: 4, y: 4 (y_hi: 2, y_lo: 2; y = y_hi * 2 + y_lo), z: 8, core: 2. Of those that a mesh axis runs over, the one named last changes fastest.
Arguments:
- front_tokens: bfloat16 [4, 4096, 2048], P('section', 'expert'), may hold values from -6 to 6
- front_experts: int32 [4, 4096, 8], P('section', 'expert'), may hold values from 0 to 63, all different within a row; in each aligned block of 64 rows (0 to 63, 64 to 127, ..., all dimensions but the last counted through in order) at most 9 rows name the same one
- front_probs: float32 [4, 4096, 8], P('section', 'expert'), may hold values from 0.05 to 1
- back_tokens: bfloat16 [4, 4096, 2048], P('section', 'expert'), may hold values from -6 to 6
- back_experts: int32 [4, 4096, 8], P('section', 'expert'), may hold values from 0 to 63, all different within a row; in each aligned block of 64 rows (0 to 63, 64 to 127, ..., all dimensions but the last counted through in order) at most 9 rows name the same one
- back_probs: float32 [4, 4096, 8], P('section', 'expert'), may hold values from 0.05 to 1
- back_grads: bfloat16 [4, 4096, 2048], P('section', 'expert'), may hold values from -6 to 6
- gate_weight: bfloat16 [4, 64, 2048, 768], P('section', 'expert'), may hold values from -0.125 to 0.125
- up_weight: bfloat16 [4, 64, 2048, 768], P('section', 'expert'), may hold values from -0.125 to 0.125
- down_weight: bfloat16 [4, 64, 768, 2048], P('section', 'expert'), may hold values from -0.21875 to 0.21875
Outputs:
- front_output: bfloat16 [4, 4096, 2048], P('section', 'expert')
- back_output: bfloat16 [4, 4096, 2048], P('section', 'expert')
The draws below stay inside these ranges and needn't reach their ends.
Inputs may be any that keep to these rules, and one draw needn't show every extreme that they name: `front_experts`: each token names 8 different experts. Among the 64 tokens of one device (aligned blocks along the token dimension, per section) no expert is named more than 9 times, and in some block some expert is named exactly 9 times. `back_experts`: each token names 8 different experts. Among the 64 tokens of one device (aligned blocks along the token dimension, per section) no expert is named more than 9 times, and in some block some expert is named exactly 9 times.
All inputs are finite; a program needn't handle non-finite values.
Results may differ from the reference program's by a relative error of at most 0.0064.
Values may be sent and summed in bfloat16 or wider, within the bound.
No kernel may reach another device: no remote copies, remote signals or barrier semaphores. Data moves between devices by JAX's collectives and lax.ppermute only.
A program may use at most 128 MiB of HBM per device.

```python
import math
import jax
import jax.numpy as jnp
import numpy as np
from jax import lax

D = 2048
FF = 768
TOP = 8
TOK_DEV = 64
EXPERTS = 64
SECTIONS = 4
TOKENS = 4096
MOST = 9


def steps_of(own_key, extent, shards, least, top_value):
    def one(position, parts):
        draws = jax.random.uniform(jax.random.fold_in(jax.random.fold_in(own_key, 6), position), (parts,), jnp.float32, least / len(shards), top_value / len(shards))
        return jnp.repeat(jnp.exp(draws), extent[position] // parts).reshape((-1,) + (1,) * (len(extent) - position - 1))

    gain = one(*shards[0])
    for cut in shards[1:]:
        gain = gain * one(*cut)
    return gain


def routed_block(rng, own, number, rows, count, top, most, lean):
    order = jax.random.permutation(rng, count)
    crowded, ordinary = portions_of(count, rows * top, most, lean, True), portions_of(count, rows * top, most, lean, False)
    places = jnp.arange(count)

    def named(lengths, turn):
        used = int((lengths > 0).sum())
        fixed = max(1, used // 4)
        shifted = fixed + (places - fixed + turn * (used - fixed)) % max(1, count - fixed)
        return jnp.zeros((count,), jnp.int32).at[order[jnp.where(places < fixed, places, shifted)]].set(jnp.asarray(lengths, jnp.int32))

    lengths = jnp.where(number % 4 == 0, named(crowded, number // 4), named(ordinary, number - number // 4 - 1))
    mixed = jax.random.permutation(jax.random.fold_in(own, 3), count)
    source_of, taker = mixed[0:count // 2 * 2:2], mixed[1:count // 2 * 2:2]
    margin = jnp.minimum(lengths[source_of] - 1, most - lengths[taker]) // 2
    margin = jnp.where((source_of == order[0]) | (taker == order[0]) | (lengths[taker] == 0), 0, jnp.maximum(margin, 0))
    shifted = jax.random.randint(jax.random.fold_in(own, 4), (count // 2,), 0, 1 << 20) % (margin + 1)
    lengths = lengths.at[source_of].add(-shifted).at[taker].add(shifted)
    members = jnp.searchsorted(jnp.cumsum(lengths), jnp.arange(rows * top), side="right").astype(jnp.int32)
    table = members.reshape(top, rows).T
    table = table[jax.random.permutation(jax.random.fold_in(own, 1), rows)]
    turn = jax.random.randint(jax.random.fold_in(own, 2), (rows, 1), 0, top)
    return jnp.take_along_axis(table, (jnp.arange(top)[None, :] + turn) % top, axis=1)


def portions_of(count, total, most, slope, full):
    portions = [(1 << 20) // math.isqrt(rank ** slope) + 1 for rank in range(1, count + 1)]
    largest = most if full else min(most, max(-(-total // count), total * portions[0] // sum(portions)))
    least = 1 if total - largest >= count - 1 else 0
    holding, surplus = [largest] + [least] * (count - 1), total - largest - least * (count - 1)
    while surplus > 0:
        free = [i for i in range(1, count) if holding[i] < largest] or [i for i in range(1, count) if holding[i] < most]
        pool, remaining = sum([portions[i] for i in free]), surplus
        for i in free:
            extra = min(most - holding[i], max(1, remaining * portions[i] // pool), surplus)
            holding[i] = holding[i] + extra
            surplus = surplus - extra
    return np.array(holding)


def scatter_about(rng, shape, spread, reach, pieces=(), kind=jnp.bfloat16):
    gain = steps_of(rng, shape, pieces, -0.22, 0.18) if pieces else 1.0
    array = jax.random.normal(rng, shape, jnp.float32) * spread * gain
    return jnp.minimum(jnp.maximum(array, -reach), reach).astype(kind)


def setup_inputs(seed: int = 0) -> dict:
    key_of = jax.random.split(jax.random.key(seed), 11)
    front_tokens = scatter_about(key_of[0], (SECTIONS, TOKENS, D), 1.0, 6.0, ((0, 4), (1, 64)))
    front_experts_keys = jax.random.split(jax.random.fold_in(key_of[1], 1), SECTIONS * TOKENS // TOK_DEV)
    front_experts_turns = jax.random.permutation(jax.random.fold_in(key_of[1], 3), SECTIONS * TOKENS // TOK_DEV)
    front_experts = jax.vmap(lambda own, number: routed_block(jax.random.fold_in(key_of[1], 2), own, number, TOK_DEV, EXPERTS, TOP, MOST, 2))(front_experts_keys, front_experts_turns).reshape((SECTIONS, TOKENS, TOP))
    front_probs = jnp.clip(jnp.exp(math.log(1.0) - 2.9957323 * jax.random.uniform(key_of[2], (SECTIONS, TOKENS, TOP), jnp.float32) ** steps_of(key_of[2], (SECTIONS, TOKENS, TOP), ((0, 4), (1, 64)), -0.2, 0.2)), 0.05, 1.0)
    back_tokens = scatter_about(key_of[3], (SECTIONS, TOKENS, D), 1.0, 6.0, ((0, 4), (1, 64)))
    back_experts_keys = jax.random.split(jax.random.fold_in(key_of[4], 1), SECTIONS * TOKENS // TOK_DEV)
    back_experts_turns = jax.random.permutation(jax.random.fold_in(key_of[4], 3), SECTIONS * TOKENS // TOK_DEV)
    back_experts = jax.vmap(lambda own, number: routed_block(jax.random.fold_in(key_of[4], 2), own, number, TOK_DEV, EXPERTS, TOP, MOST, 2))(back_experts_keys, back_experts_turns).reshape((SECTIONS, TOKENS, TOP))
    back_probs = jnp.clip(jnp.exp(math.log(1.0) - 2.9957323 * jax.random.uniform(key_of[5], (SECTIONS, TOKENS, TOP), jnp.float32) ** steps_of(key_of[5], (SECTIONS, TOKENS, TOP), ((0, 4), (1, 64)), -0.2, 0.2)), 0.05, 1.0)
    back_grads = scatter_about(key_of[6], (SECTIONS, TOKENS, D), 1.0, 6.0, ((0, 4), (1, 64)))
    gate_weight = scatter_about(key_of[7], (SECTIONS, EXPERTS, D, FF), D ** -0.5, 0.125, ((0, 4), (1, 64)))
    up_weight = scatter_about(key_of[8], (SECTIONS, EXPERTS, D, FF), D ** -0.5, 0.125, ((0, 4), (1, 64)))
    down_weight = scatter_about(key_of[9], (SECTIONS, EXPERTS, FF, D), FF ** -0.5, 0.21875, ((0, 4), (1, 64)))
    return dict(front_tokens=front_tokens, front_experts=front_experts, front_probs=front_probs, back_tokens=back_tokens, back_experts=back_experts, back_probs=back_probs, back_grads=back_grads, gate_weight=gate_weight, up_weight=up_weight, down_weight=down_weight)


def shares_of(probs):
    return probs / jnp.sum(probs, axis=-1, keepdims=True)


def forward_rows(rows, gate_matrix, up_matrix, down_matrix):
    gate = jnp.dot(rows, gate_matrix, preferred_element_type=jnp.float32)
    upper = jnp.dot(rows, up_matrix, preferred_element_type=jnp.float32)
    hidden = (gate * jax.nn.sigmoid(gate) * upper).astype(jnp.bfloat16)
    return jnp.dot(hidden, down_matrix, preferred_element_type=jnp.float32).astype(jnp.bfloat16)


def backward_rows(rows, grads, gate_matrix, up_matrix, down_matrix):
    gate = jnp.dot(rows, gate_matrix, preferred_element_type=jnp.float32)
    upper = jnp.dot(rows, up_matrix, preferred_element_type=jnp.float32)
    sigma = jax.nn.sigmoid(gate)
    hidden_grad = jnp.dot(grads, down_matrix.T, preferred_element_type=jnp.float32)
    gate_grad = (hidden_grad * upper * sigma * (1.0 + gate * (1.0 - sigma))).astype(jnp.bfloat16)
    upper_grad = (hidden_grad * gate * sigma).astype(jnp.bfloat16)
    summed = jnp.dot(gate_grad, gate_matrix.T, preferred_element_type=jnp.float32)
    summed = summed + jnp.dot(upper_grad, up_matrix.T, preferred_element_type=jnp.float32)
    return summed.astype(jnp.bfloat16)


def section_layer(front_tokens, front_experts, front_probs, back_tokens, back_experts, back_probs, back_grads, gate_weight, up_weight, down_weight):
    limit = EXPERTS * MOST
    front_flat = front_experts.reshape(-1)
    back_flat = back_experts.reshape(-1)
    front_share = shares_of(front_probs).reshape(-1)
    back_share = shares_of(back_probs).reshape(-1)
    positions = jnp.arange(limit, dtype=jnp.int32)

    def select(flat, expert):
        match = flat == expert
        (index,) = jnp.nonzero(match, size=limit, fill_value=0)
        index = index.astype(jnp.int32)
        live = positions < jnp.sum(match.astype(jnp.int32))
        return index, live

    def one_expert(carry, inputs):
        front_total, back_total = carry
        expert, gate_matrix, up_matrix, down_matrix = inputs
        index, live = select(front_flat, expert)
        owner = index // TOP
        produced = forward_rows(front_tokens[owner], gate_matrix, up_matrix, down_matrix)
        factor = jnp.where(live, front_share[index], jnp.float32(0.0))
        front_total = front_total.at[owner].add(factor[:, None] * produced.astype(jnp.float32))
        index, live = select(back_flat, expert)
        owner = index // TOP
        grads = (back_share[index][:, None] * back_grads[owner].astype(jnp.float32)).astype(jnp.bfloat16)
        produced = backward_rows(back_tokens[owner], grads, gate_matrix, up_matrix, down_matrix)
        factor = live.astype(jnp.float32)
        back_total = back_total.at[owner].add(factor[:, None] * produced.astype(jnp.float32))
        return (front_total, back_total), None

    start = (jnp.zeros((TOKENS, D), jnp.float32), jnp.zeros((TOKENS, D), jnp.float32))
    labels = jnp.arange(EXPERTS, dtype=jnp.int32)
    (front_total, back_total), ignored = lax.scan(one_expert, start, (labels, gate_weight, up_weight, down_weight))
    return front_total.astype(jnp.bfloat16), back_total.astype(jnp.bfloat16)


def reference(front_tokens, front_experts, front_probs, back_tokens, back_experts, back_probs, back_grads, gate_weight, up_weight, down_weight):
    front_list = []
    back_list = []
    for section in range(SECTIONS):
        front_part, back_part = section_layer(front_tokens[section], front_experts[section], front_probs[section], back_tokens[section], back_experts[section], back_probs[section], back_grads[section], gate_weight[section], up_weight[section], down_weight[section])
        front_list.append(front_part)
        back_list.append(back_part)
    front_output = jnp.roll(jnp.stack(front_list), 1, axis=0)
    back_output = jnp.roll(jnp.stack(back_list), -1, axis=0)
    return front_output, back_output
```

```python
import functools

import jax
import jax.numpy as jnp
from jax import lax
from jax.experimental import pallas as pl
from jax.experimental.pallas import tpu as pltpu
from jax.sharding import Mesh, PartitionSpec as P

MOST = 9
DEPTH, WIDE, LONG = 8, 2, 4
EXPERTS = WIDE * LONG
EACH = DEPTH * MOST
SLOTS = EXPERTS * EACH
ORDER = (0, 4, 3, 5, 2, 6, 1, 7)
LANES = 128
MIB = 1024 * 1024


def along(block, distance, hop=0):
    n = lax.axis_size("section")
    route = []
    for s in range(n):
        for z in range(DEPTH):
            route.append((s * DEPTH + z, (s + hop) % n * DEPTH + (z + distance) % DEPTH))
    return lax.ppermute(block, ("section", "z"), route)


def after(block, *others):
    return lax.optimization_barrier((block,) + others)[0]


def ends(up, down):
    half = up.shape[0] // 2
    return [along(up[:half], 1), along(down[half:], -1)]


def gathered(block, early, late):
    block = after(block, *early)
    up1, down1 = along(block, 1), along(block, -1)
    up2, down2 = along(up1, 1), along(down1, -1)
    up2, down2 = after(up2, *late), after(down2, *late)
    up3, down3 = along(up2, 1), along(down2, -1)
    return [block, up1, up2, up3] + ends(up3, down3) + [down3, down2, down1]


def gathered_pair(a, b):
    ups, downs = [a], [a]
    others_up, others_down = [b], [b]
    for step in range(1, DEPTH // 2):
        up, down = ups[-1], downs[-1]
        if step > 2:
            other = (others_up[step - 2], others_down[step - 2])
            up, down = after(up, *other), after(down, *other)
        ups.append(along(up, 1))
        downs.append(along(down, -1))
        others_up.append(along(others_up[-1], 1))
        others_down.append(along(others_down[-1], -1))
    other = (others_up[2], others_down[2])
    last = ends(after(ups[3], *other), after(downs[3], *other))
    last[0] = after(last[0], others_up[3], others_down[3])
    first = ups + last + downs[:0:-1]
    second = others_up + ends(others_up[3], others_down[3]) + others_down[:0:-1]
    return first, second


def halves(middle, low3, high3):
    half = middle.shape[0] // 2
    down, up = along(middle[:half], -1), along(middle[half:], 1)
    came = (low3[:half] + down.astype(jnp.float32)).astype(jnp.bfloat16)
    rose = (high3[half:] + up.astype(jnp.float32)).astype(jnp.bfloat16)
    low3 = jnp.concatenate([came, low3[half:].astype(jnp.bfloat16)])
    high3 = jnp.concatenate([high3[:half].astype(jnp.bfloat16), rose])
    return low3, high3


def returned(parts, hop, direct):
    own, middle, low3, high3, low2, high2, low1, high1 = parts
    lone = [along(own, 0, hop)]
    if direct:
        lone.append(along(middle, DEPTH // 2, hop))
        low3, high3 = low3.astype(jnp.bfloat16), high3.astype(jnp.bfloat16)
    else:
        low3, high3 = halves(middle, low3, high3)
    down, up = along(low3, -1), along(high3, 1)
    low2 = (low2 + down.astype(jnp.float32)).astype(jnp.bfloat16)
    high2 = (high2 + up.astype(jnp.float32)).astype(jnp.bfloat16)
    down, up = along(low2, -1), along(high2, 1)
    low1 = (low1 + down.astype(jnp.float32)).astype(jnp.bfloat16)
    high1 = (high1 + up.astype(jnp.float32)).astype(jnp.bfloat16)
    before = [low1, high1] + lone
    down, up = along(low1, -1, hop), along(high1, 1, hop)
    total = sum(one.astype(jnp.float32) for one in lone + [down, up])
    return total.astype(jnp.bfloat16), before


def dot(a, b):
    return jnp.dot(a, b, preferred_element_type=jnp.float32)


def dot_t(a, b):
    return lax.dot_general(a, b, (((1,), (1,)), ((), ())), preferred_element_type=jnp.float32)


def split3(value):
    high = value.astype(jnp.bfloat16)
    value = value - high.astype(jnp.float32)
    middle = value.astype(jnp.bfloat16)
    value = value - middle.astype(jnp.float32)
    return high, middle, value.astype(jnp.bfloat16)


def bits(mask):
    return jnp.where(mask, 1.0, 0.0).astype(jnp.bfloat16)


def make_plan(meta, plane):
    square = (LANES, LANES)
    i = lax.broadcasted_iota(jnp.int32, square, 0)
    c = lax.broadcasted_iota(jnp.int32, square, 1)
    side, pick, kind = c >> 6, (c >> 3) & 7, c & 7
    probs = (i >= 16 + side * 24) & (i < 40 + side * 24)
    chosen = dot(meta, bits(i == side * 8 + pick))
    prob = dot(meta, bits(probs & ((i & 7) == pick)))
    whole = dot(meta, bits(probs))
    shape = chosen.shape
    lane = lax.broadcasted_iota(jnp.int32, shape, 1)
    label = (plane * EXPERTS + (lane & 7)).astype(jnp.float32)
    hit = chosen == label
    pairs = bits((c < 16) & ((i & 7) == (c & 7)) & ((i >> 6) == (c >> 3)))
    named = dot(bits(hit), pairs)
    share = jnp.where(hit, prob / whole, 0.0)
    share = sum(dot(part, pairs) for part in split3(share))
    rows = shape[0]
    a = lax.broadcasted_iota(jnp.int32, (rows, rows), 0)
    b = lax.broadcasted_iota(jnp.int32, (rows, rows), 1)
    earlier = bits((b < a) & ((a >> 6) == (b >> 6)))
    rank = dot(earlier, named.astype(jnp.bfloat16)).astype(jnp.int32)
    row = lax.broadcasted_iota(jnp.int32, shape, 0)
    column = (lane & 7) * EACH + (row >> 6) * MOST + rank
    return jnp.where(named > 0.5, column, -1), share


def spread_tiles(column, share, side):
    tiles = []
    for start in range(0, SLOTS, LANES):
        stop = min(start + LANES, SLOTS)
        shape = (column.shape[0], stop - start)
        slot = lax.broadcasted_iota(jnp.int32, shape, 1) + start
        total = jnp.zeros(shape, jnp.float32)
        for j in range(start // EACH, -(-stop // EACH)):
            lane = side * EXPERTS + j
            value = 1.0 if share is None else share[:, lane : lane + 1]
            total = jnp.where(slot == column[:, lane : lane + 1], value, total)
        tiles.append((start, stop, total))
    return tiles


def fill(tables, column, share, side, turned):
    for start, stop, tile in spread_tiles(column, share, side):
        if turned:
            tile = tile.T
        for table in tables:
            part = tile.astype(jnp.bfloat16)
            tile = tile - part.astype(jnp.float32)
            if turned:
                table[start:stop, :] = part
            else:
                table[:, start:stop] = part


def first_kernel(*refs):
    n = DEPTH + 1
    plane_ref, pieces, metas = refs[0], refs[1 : 1 + n], refs[1 + n : 1 + 2 * n]
    rows_ref, column_ref, share_ref, table, stack = refs[1 + 2 * n :]

    @pl.when(pl.program_id(0) == 0)
    def _():
        meta = jnp.concatenate([ref[...] for ref in metas], axis=0)
        column, share = make_plan(meta, plane_ref[0])
        column_ref[...] = column
        share_ref[...] = share
        fill([table], column, None, 1, True)

    at = 0
    for ref in pieces:
        stack[at : at + ref.shape[0], :] = ref[...]
        at += ref.shape[0]
    rows_ref[...] = dot(table[...], stack[...]).astype(jnp.bfloat16)


def place_kernel(side, weighted, n, *refs):
    pieces, column_ref, share_ref = refs[:n], refs[n], refs[n + 1]
    rows_ref, tables, stack = refs[n + 2], refs[n + 3 : -1], refs[-1]

    @pl.when(pl.program_id(0) == 0)
    def _():
        fill(tables, column_ref[...], share_ref[...] if weighted else None, side, True)

    at = 0
    for ref in pieces:
        stack[at : at + ref.shape[0], :] = ref[...]
        at += ref.shape[0]
    rows_ref[...] = sum(dot(table[...], stack[...]) for table in tables).astype(jnp.bfloat16)


def weigh_kernel(sides, column_ref, share_ref, *tables):
    for side, weighted in sides:
        count = 2 if weighted else 1
        share = share_ref[...] if weighted else None
        fill(tables[:count], column_ref[...], share, side, False)
        tables = tables[count:]


def combine_kernel(count, rows_ref, *refs):
    tables, outs = refs[:count], refs[count:]
    rows = rows_ref[...]
    total = sum(dot(table[...], rows) for table in tables)
    tokens = total.shape[0] // DEPTH
    for k, ref in zip(ORDER, outs):
        ref[...] = total[k * tokens : (k + 1) * tokens].astype(ref.dtype)


def pack_kernel(fe_ref, fp_ref, be_ref, bp_ref, rows_ref, out_ref):
    width = rows_ref.shape[1]
    out_ref[:, :width] = rows_ref[...]
    parts = [fe_ref[...].astype(jnp.float32), be_ref[...].astype(jnp.float32)]
    for ref in (fp_ref, bp_ref):
        parts += [part.astype(jnp.float32) for part in split3(ref[...])]
    used = sum(part.shape[0] for part in parts)
    parts.append(jnp.zeros((LANES - used, parts[0].shape[1]), jnp.float32))
    out_ref[:, width:] = jnp.concatenate(parts, axis=0).T.astype(jnp.bfloat16)


def pack(front_experts, front_probs, back_experts, back_probs, rows):
    tokens, width = rows.shape
    inputs = (front_experts.T, front_probs.T, back_experts.T, back_probs.T, rows)
    return pl.pallas_call(
        pack_kernel,
        out_shape=jax.ShapeDtypeStruct((tokens, width + LANES), jnp.bfloat16),
        compiler_params=pltpu.CompilerParams(vmem_limit_bytes=24 * MIB),
        name="pack",
    )(*in_hbm(inputs))


STEPS = 2


def in_hbm(arrays):
    return [pltpu.with_memory_space_constraint(array, pltpu.HBM) for array in arrays]


def params(limit):
    return pltpu.CompilerParams(vmem_limit_bytes=limit * MIB, dimension_semantics=("arbitrary",))


def piece_specs(pieces, width, start=0):
    at = start // (width // STEPS)
    return [pl.BlockSpec((p.shape[0], width // STEPS), lambda i: (0, i + at)) for p in pieces]


def whole_spec(shape):
    return pl.BlockSpec(shape, lambda i: (0, 0))


def first_place(pieces, width):
    tokens = sum(p.shape[0] for p in pieces)
    slots = EXPERTS * EACH
    last = pieces[0].shape[1] // LANES - 1
    metas = [pl.BlockSpec((p.shape[0], LANES), lambda i: (0, last)) for p in pieces]
    plan = (tokens, LANES)
    return pl.pallas_call(
        first_kernel,
        grid=(STEPS,),
        in_specs=[pl.BlockSpec(memory_space=pltpu.SMEM)] + piece_specs(pieces, width) + metas,
        out_specs=[
            pl.BlockSpec((slots, width // STEPS), lambda i: (0, i)),
            whole_spec(plan),
            whole_spec(plan),
        ],
        out_shape=[
            pltpu.HBM((slots, width), jnp.bfloat16),
            pltpu.HBM(plan, jnp.int32),
            pltpu.HBM(plan, jnp.float32),
        ],
        scratch_shapes=[
            pltpu.VMEM((slots, tokens), jnp.bfloat16),
            pltpu.VMEM((tokens, width // STEPS), jnp.bfloat16),
        ],
        compiler_params=params(24),
        cost_estimate=pl.CostEstimate(
            flops=2 * slots * tokens * width, bytes_accessed=6 * MIB, transcendentals=0
        ),
        name="first_place",
    )(lax.axis_index("z").astype(jnp.int32).reshape(1), *in_hbm(pieces), *in_hbm(pieces))


def place(pieces, column, share, side, weighted, width, start=0):
    tokens = sum(p.shape[0] for p in pieces)
    slots = EXPERTS * EACH
    count = 2 if weighted else 1
    return pl.pallas_call(
        functools.partial(place_kernel, side, weighted, len(pieces)),
        grid=(STEPS,),
        in_specs=piece_specs(pieces, width, start) + [whole_spec(column.shape)] * 2,
        out_specs=pl.BlockSpec((slots, width // STEPS), lambda i: (0, i)),
        out_shape=pltpu.HBM((slots, width), jnp.bfloat16),
        scratch_shapes=[pltpu.VMEM((slots, tokens), jnp.bfloat16)] * count
        + [pltpu.VMEM((tokens, width // STEPS), jnp.bfloat16)],
        compiler_params=params(24),
        cost_estimate=pl.CostEstimate(
            flops=2 * count * slots * tokens * width, bytes_accessed=6 * MIB, transcendentals=0
        ),
        name="place",
    )(*in_hbm(pieces + [column, share]))


def weigh(column, share):
    sides = ((1, False), (0, True))
    table = jax.ShapeDtypeStruct((column.shape[0], SLOTS), jnp.bfloat16)
    return pl.pallas_call(
        functools.partial(weigh_kernel, sides),
        out_shape=[pltpu.HBM(table.shape, table.dtype)] * 3,
        compiler_params=pltpu.CompilerParams(vmem_limit_bytes=24 * MIB),
        cost_estimate=pl.CostEstimate(flops=0, bytes_accessed=2 * MIB, transcendentals=0),
        name="weigh",
    )(*in_hbm((column, share)))


def combine(rows, tables, direct):
    slots, width = rows.shape
    tokens = tables[0].shape[0]
    each = tokens // DEPTH
    sent = 4 if direct else 2
    return pl.pallas_call(
        functools.partial(combine_kernel, len(tables)),
        grid=(STEPS,),
        in_specs=[pl.BlockSpec((slots, width // STEPS), lambda i: (0, i))]
        + [whole_spec(table.shape) for table in tables],
        out_specs=[pl.BlockSpec((each, width // STEPS), lambda i: (0, i))] * DEPTH,
        out_shape=[jax.ShapeDtypeStruct((each, width), jnp.bfloat16)] * sent
        + [pltpu.HBM((each, width), jnp.float32)] * (DEPTH - sent),
        compiler_params=params(24),
        cost_estimate=pl.CostEstimate(
            flops=2 * len(tables) * slots * tokens * width,
            bytes_accessed=6 * MIB,
            transcendentals=0,
        ),
        name="combine",
    )(rows, *in_hbm(tables))


def front_kernel(rows_ref, gate_ref, up_ref, down_ref, out_ref, total):
    step = pl.program_id(0)
    rows = rows_ref[...]
    gate = dot(rows, gate_ref[...])
    upper = dot(rows, up_ref[...])
    hidden = (gate * jax.nn.sigmoid(gate) * upper).astype(jnp.bfloat16)
    produced = dot(hidden, down_ref[...])

    @pl.when(step == 0)
    def _():
        total[...] = produced

    @pl.when(step > 0)
    def _():
        total[...] += produced

    @pl.when(step == pl.num_programs(0) - 1)
    def _():
        out_ref[...] = total[...].astype(jnp.bfloat16)


def back_kernel(rows_ref, grads_ref, gate_ref, up_ref, down_ref, out_ref, total):
    step = pl.program_id(0)
    rows = rows_ref[...]
    gate = dot(rows, gate_ref[...])
    upper = dot(rows, up_ref[...])
    sigma = jax.nn.sigmoid(gate)
    hidden_grad = dot_t(grads_ref[...], down_ref[...])
    gate_grad = (hidden_grad * upper * sigma * (1.0 + gate * (1.0 - sigma))).astype(jnp.bfloat16)
    upper_grad = (hidden_grad * gate * sigma).astype(jnp.bfloat16)
    produced = dot_t(gate_grad, gate_ref[...]) + dot_t(upper_grad, up_ref[...])

    @pl.when(step == 0)
    def _():
        total[...] = produced

    @pl.when(step > 0)
    def _():
        total[...] += produced

    @pl.when(step == pl.num_programs(0) - 1)
    def _():
        out_ref[...] = total[...].astype(jnp.bfloat16)


def expert(kernel, inputs, gate_matrix, up_matrix, down_matrix, products, name):
    width, units = gate_matrix.shape
    slots = inputs[0].shape[0]
    cut = 256
    tall = pl.BlockSpec((width, cut), lambda i: (0, i))
    flat = pl.BlockSpec((cut, width), lambda i: (i, 0))
    return pl.pallas_call(
        kernel,
        grid=(units // cut,),
        in_specs=[whole_spec(inputs[0].shape)] * len(inputs) + [tall, tall, flat],
        out_specs=whole_spec(inputs[0].shape),
        out_shape=pltpu.HBM(inputs[0].shape, jnp.bfloat16),
        scratch_shapes=[pltpu.VMEM((slots, width), jnp.float32)],
        compiler_params=params(40),
        cost_estimate=pl.CostEstimate(
            flops=2 * products * slots * width * units,
            bytes_accessed=16 * MIB,
            transcendentals=slots * units,
        ),
        name=name,
    )(*inputs, *in_hbm((gate_matrix, up_matrix, down_matrix)))


def exchange(rows):
    split = rows.reshape(EXPERTS, EACH, rows.shape[1])
    split = lax.all_to_all(split, ("y", "x"), split_axis=0, concat_axis=0, tiled=True)
    return split.reshape(rows.shape)


def local(
    front_tokens,
    front_experts,
    front_probs,
    back_tokens,
    back_experts,
    back_probs,
    back_grads,
    gate_weight,
    up_weight,
    down_weight,
):
    weights = (gate_weight[0, 0], up_weight[0, 0], down_weight[0, 0])
    width = back_tokens.shape[2]
    packed = pack(front_experts[0], front_probs[0], back_experts[0], back_probs[0], back_tokens[0])
    first, grads_all = gathered_pair(packed, back_grads[0])
    placed, column, share = first_place(first, width)
    back_rows = exchange(placed)
    front_all = gathered(front_tokens[0], (placed,), (back_rows,))
    placed = place(grads_all, column, share, 1, True, width)
    grad_rows = exchange(after(placed, front_all[2], front_all[7]))
    placed = place(front_all, column, share, 0, False, width)
    front_rows = exchange(placed)

    grad_rows = after(grad_rows, placed)
    produced = expert(back_kernel, (back_rows, grad_rows), *weights, 5, "back")
    back_home = exchange(after(produced, front_rows))
    back_table, *front_tables = weigh(column, share)
    front_rows = after(front_rows, back_table)
    produced = expert(front_kernel, (front_rows,), *weights, 3, "front")
    back_home = after(back_home, produced)
    front_home = exchange(produced)

    input_grad, sent = returned(combine(back_home, [back_table], True), -1, True)
    front_home = after(front_home, *sent)
    layer_out, _ = returned(combine(front_home, front_tables, False), 1, False)
    return layer_out[None], input_grad[None]


def solution(mesh):
    fine = Mesh(mesh.devices.reshape(4, DEPTH, WIDE, LONG), ("section", "z", "y", "x"))
    split = ("z", "y", "x")
    data = P("section", split, None)
    weight = P("section", split, None, None)
    return jax.shard_map(
        local,
        mesh=fine,
        in_specs=(data,) * 7 + (weight,) * 3,
        out_specs=(data, data),
        check_vma=False,
    )
```

```python
import functools

import jax
import jax.numpy as jnp
from jax import lax
from jax.experimental import pallas as pl
from jax.experimental.pallas import tpu as pltpu
from jax.sharding import Mesh, PartitionSpec as P

MOST = 9
DEPTH, WIDE, LONG = 8, 2, 4
EXPERTS = WIDE * LONG
EACH = DEPTH * MOST
SLOTS = EXPERTS * EACH
ORDER = (0, 4, 3, 5, 2, 6, 1, 7)
LANES = 128
MIB = 1024 * 1024


def along(block, distance, hop=0):
    n = lax.axis_size("section")
    route = []
    for s in range(n):
        for z in range(DEPTH):
            route.append((s * DEPTH + z, (s + hop) % n * DEPTH + (z + distance) % DEPTH))
    return lax.ppermute(block, ("section", "z"), route)


def after(block, *others):
    return lax.optimization_barrier((block,) + others)[0]


def ends(up, down):
    half = up.shape[0] // 2
    return [along(up[:half], 1), along(down[half:], -1)]


def gathered(block, early, late):
    block = after(block, *early)
    up1, down1 = along(block, 1), along(block, -1)
    up1, down1 = after(up1, *late), after(down1, *late)
    up2, down2 = along(up1, 1), along(down1, -1)
    up3, down3 = along(up2, 1), along(down2, -1)
    return [block, up1, up2, up3] + ends(up3, down3) + [down3, down2, down1]


def gathered_pair(a, b):
    ups, downs = [a], [a]
    others_up, others_down = [b], [b]
    for step in range(1, DEPTH // 2):
        up, down = ups[-1], downs[-1]
        if step == 3:
            other = (others_up[2], others_down[2])
            up, down = after(up, *other), after(down, *other)
        ups.append(along(up, 1))
        downs.append(along(down, -1))
        others_up.append(along(others_up[-1], 1))
        others_down.append(along(others_down[-1], -1))
    first = ups + ends(ups[3], downs[3]) + downs[:0:-1]
    second = others_up + ends(others_up[3], others_down[3]) + others_down[:0:-1]
    return first, second


def returned(parts, hop, wait_for=()):
    own, middle, low3, high3, low2, high2, low1, high1 = parts
    half = middle.shape[0] // 2
    down, up = along(middle[:half], -1), along(middle[half:], 1)
    down = jnp.pad(down.astype(jnp.float32), ((0, half), (0, 0)))
    up = jnp.pad(up.astype(jnp.float32), ((half, 0), (0, 0)))
    low3 = (low3 + down).astype(jnp.bfloat16)
    high3 = (high3 + up).astype(jnp.bfloat16)
    down, up = along(low3, -1), along(high3, 1)
    low2 = (low2 + down.astype(jnp.float32)).astype(jnp.bfloat16)
    high2 = (high2 + up.astype(jnp.float32)).astype(jnp.bfloat16)
    down, up = along(low2, -1), along(high2, 1)
    came = (down, up)
    low1 = (low1 + down.astype(jnp.float32)).astype(jnp.bfloat16)
    high1 = (high1 + up.astype(jnp.float32)).astype(jnp.bfloat16)
    if wait_for:
        low1, high1 = after(low1, *wait_for), after(high1, *wait_for)
    down, up = along(low1, -1, hop), along(high1, 1, hop)
    total = sum(one.astype(jnp.float32) for one in (along(own, 0, hop), down, up))
    return total.astype(jnp.bfloat16), came


def dot(a, b):
    return jnp.dot(a, b, preferred_element_type=jnp.float32)


def dot_t(a, b):
    return lax.dot_general(a, b, (((1,), (1,)), ((), ())), preferred_element_type=jnp.float32)


def split3(value):
    high = value.astype(jnp.bfloat16)
    value = value - high.astype(jnp.float32)
    middle = value.astype(jnp.bfloat16)
    value = value - middle.astype(jnp.float32)
    return high, middle, value.astype(jnp.bfloat16)


def bits(mask):
    return jnp.where(mask, 1.0, 0.0).astype(jnp.bfloat16)


def make_plan(meta, plane):
    square = (LANES, LANES)
    i = lax.broadcasted_iota(jnp.int32, square, 0)
    c = lax.broadcasted_iota(jnp.int32, square, 1)
    side, pick, kind = c >> 6, (c >> 3) & 7, c & 7
    probs = (i >= 16 + side * 24) & (i < 40 + side * 24)
    chosen = dot(meta, bits(i == side * 8 + pick))
    prob = dot(meta, bits(probs & ((i & 7) == pick)))
    whole = dot(meta, bits(probs))
    shape = chosen.shape
    lane = lax.broadcasted_iota(jnp.int32, shape, 1)
    label = (plane * EXPERTS + (lane & 7)).astype(jnp.float32)
    hit = chosen == label
    pairs = bits((c < 16) & ((i & 7) == (c & 7)) & ((i >> 6) == (c >> 3)))
    named = dot(bits(hit), pairs)
    share = jnp.where(hit, prob / whole, 0.0)
    share = sum(dot(part, pairs) for part in split3(share))
    rows = shape[0]
    a = lax.broadcasted_iota(jnp.int32, (rows, rows), 0)
    b = lax.broadcasted_iota(jnp.int32, (rows, rows), 1)
    earlier = bits((b < a) & ((a >> 6) == (b >> 6)))
    rank = dot(earlier, named.astype(jnp.bfloat16)).astype(jnp.int32)
    row = lax.broadcasted_iota(jnp.int32, shape, 0)
    column = (lane & 7) * EACH + (row >> 6) * MOST + rank
    return jnp.where(named > 0.5, column, -1), share


def spread_tiles(column, share, side):
    tiles = []
    for start in range(0, SLOTS, LANES):
        stop = min(start + LANES, SLOTS)
        shape = (column.shape[0], stop - start)
        slot = lax.broadcasted_iota(jnp.int32, shape, 1) + start
        total = jnp.zeros(shape, jnp.float32)
        for j in range(start // EACH, -(-stop // EACH)):
            lane = side * EXPERTS + j
            value = 1.0 if share is None else share[:, lane : lane + 1]
            total = jnp.where(slot == column[:, lane : lane + 1], value, total)
        tiles.append((start, stop, total))
    return tiles


def fill(tables, column, share, side, turned):
    for start, stop, tile in spread_tiles(column, share, side):
        if turned:
            tile = tile.T
        for table in tables:
            part = tile.astype(jnp.bfloat16)
            tile = tile - part.astype(jnp.float32)
            if turned:
                table[start:stop, :] = part
            else:
                table[:, start:stop] = part


def first_kernel(*refs):
    n = DEPTH + 1
    plane_ref, pieces, metas = refs[0], refs[1 : 1 + n], refs[1 + n : 1 + 2 * n]
    rows_ref, column_ref, share_ref, table, stack = refs[1 + 2 * n :]

    @pl.when(pl.program_id(0) == 0)
    def _():
        meta = jnp.concatenate([ref[...] for ref in metas], axis=0)
        column, share = make_plan(meta, plane_ref[0])
        column_ref[...] = column
        share_ref[...] = share
        fill([table], column, None, 1, True)

    at = 0
    for ref in pieces:
        stack[at : at + ref.shape[0], :] = ref[...]
        at += ref.shape[0]
    rows_ref[...] = dot(table[...], stack[...]).astype(jnp.bfloat16)


def place_kernel(side, weighted, n, *refs):
    pieces, column_ref, share_ref = refs[:n], refs[n], refs[n + 1]
    rows_ref, table, factor, stack = refs[n + 2 :]

    @pl.when(pl.program_id(0) == 0)
    def _():
        if weighted:
            for start, stop, tile in spread_tiles(column_ref[...], share_ref[...], side):
                tile = tile.T
                table[start:stop, :] = bits(tile > 0.0)
                factor[start:stop, :] = jnp.sum(tile, axis=1, keepdims=True)
        else:
            fill([table], column_ref[...], None, side, True)

    at = 0
    for ref in pieces:
        stack[at : at + ref.shape[0], :] = ref[...]
        at += ref.shape[0]
    rows = dot(table[...], stack[...])
    if weighted:
        rows = rows * factor[...]
    rows_ref[...] = rows.astype(jnp.bfloat16)


def weigh_kernel(sides, column_ref, share_ref, *tables):
    for side, weighted in sides:
        count = 2 if weighted else 1
        share = share_ref[...] if weighted else None
        fill(tables[:count], column_ref[...], share, side, False)
        tables = tables[count:]


def combine_kernel(count, rows_ref, *refs):
    tables, outs = refs[:count], refs[count:]
    rows = rows_ref[...]
    total = sum(dot(table[...], rows) for table in tables)
    tokens = total.shape[0] // DEPTH
    for k, ref in zip(ORDER, outs):
        ref[...] = total[k * tokens : (k + 1) * tokens].astype(ref.dtype)


def pack_kernel(fe_ref, fp_ref, be_ref, bp_ref, rows_ref, out_ref):
    width = rows_ref.shape[1]
    out_ref[:, :width] = rows_ref[...]
    parts = [fe_ref[...].astype(jnp.float32), be_ref[...].astype(jnp.float32)]
    for ref in (fp_ref, bp_ref):
        parts += [part.astype(jnp.float32) for part in split3(ref[...])]
    used = sum(part.shape[0] for part in parts)
    parts.append(jnp.zeros((LANES - used, parts[0].shape[1]), jnp.float32))
    out_ref[:, width:] = jnp.concatenate(parts, axis=0).T.astype(jnp.bfloat16)


def pack(front_experts, front_probs, back_experts, back_probs, rows):
    tokens, width = rows.shape
    inputs = (front_experts.T, front_probs.T, back_experts.T, back_probs.T, rows)
    return pl.pallas_call(
        pack_kernel,
        out_shape=jax.ShapeDtypeStruct((tokens, width + LANES), jnp.bfloat16),
        compiler_params=pltpu.CompilerParams(vmem_limit_bytes=24 * MIB),
        name="pack",
    )(*in_hbm(inputs))


STEPS, FINE = 2, 2


def in_hbm(arrays):
    return [pltpu.with_memory_space_constraint(array, pltpu.HBM) for array in arrays]


def params(limit):
    return pltpu.CompilerParams(vmem_limit_bytes=limit * MIB, dimension_semantics=("arbitrary",))


def piece_specs(pieces, width, start=0):
    at = start // (width // STEPS)
    return [pl.BlockSpec((p.shape[0], width // STEPS), lambda i: (0, i + at)) for p in pieces]


def whole_spec(shape):
    return pl.BlockSpec(shape, lambda i: (0, 0))


def first_place(pieces, width):
    tokens = sum(p.shape[0] for p in pieces)
    slots = EXPERTS * EACH
    last = pieces[0].shape[1] // LANES - 1
    metas = [pl.BlockSpec((p.shape[0], LANES), lambda i: (0, last)) for p in pieces]
    plan = (tokens, LANES)
    return pl.pallas_call(
        first_kernel,
        grid=(STEPS,),
        in_specs=[pl.BlockSpec(memory_space=pltpu.SMEM)] + piece_specs(pieces, width) + metas,
        out_specs=[
            pl.BlockSpec((slots, width // STEPS), lambda i: (0, i)),
            whole_spec(plan),
            whole_spec(plan),
        ],
        out_shape=[
            pltpu.HBM((slots, width), jnp.bfloat16),
            pltpu.HBM(plan, jnp.int32),
            pltpu.HBM(plan, jnp.float32),
        ],
        scratch_shapes=[
            pltpu.VMEM((slots, tokens), jnp.bfloat16),
            pltpu.VMEM((tokens, width // STEPS), jnp.bfloat16),
        ],
        compiler_params=params(24),
        cost_estimate=pl.CostEstimate(
            flops=2 * slots * tokens * width, bytes_accessed=6 * MIB, transcendentals=0
        ),
        name="first_place",
    )(lax.axis_index("z").astype(jnp.int32).reshape(1), *in_hbm(pieces), *in_hbm(pieces))


def place(pieces, column, share, side, weighted, width, start=0):
    tokens = sum(p.shape[0] for p in pieces)
    slots = EXPERTS * EACH
    return pl.pallas_call(
        functools.partial(place_kernel, side, weighted, len(pieces)),
        grid=(STEPS,),
        in_specs=piece_specs(pieces, width, start) + [whole_spec(column.shape)] * 2,
        out_specs=pl.BlockSpec((slots, width // STEPS), lambda i: (0, i)),
        out_shape=pltpu.HBM((slots, width), jnp.bfloat16),
        scratch_shapes=[
            pltpu.VMEM((slots, tokens), jnp.bfloat16),
            pltpu.VMEM((slots, 1), jnp.float32),
            pltpu.VMEM((tokens, width // STEPS), jnp.bfloat16),
        ],
        compiler_params=params(24),
        cost_estimate=pl.CostEstimate(
            flops=2 * slots * tokens * width, bytes_accessed=6 * MIB, transcendentals=0
        ),
        name="place",
    )(*in_hbm(pieces + [column, share]))


def weigh(column, share):
    sides = ((1, False), (0, True))
    table = jax.ShapeDtypeStruct((column.shape[0], SLOTS), jnp.bfloat16)
    return pl.pallas_call(
        functools.partial(weigh_kernel, sides),
        out_shape=[pltpu.HBM(table.shape, table.dtype)] * 3,
        compiler_params=pltpu.CompilerParams(vmem_limit_bytes=24 * MIB),
        cost_estimate=pl.CostEstimate(flops=0, bytes_accessed=2 * MIB, transcendentals=0),
        name="weigh",
    )(*in_hbm((column, share)))


def combine(rows, tables):
    slots, width = rows.shape
    tokens = tables[0].shape[0]
    each = tokens // DEPTH
    sent = 2
    return pl.pallas_call(
        functools.partial(combine_kernel, len(tables)),
        grid=(FINE,),
        in_specs=[pl.BlockSpec((slots, width // FINE), lambda i: (0, i))]
        + [whole_spec(table.shape) for table in tables],
        out_specs=[pl.BlockSpec((each, width // FINE), lambda i: (0, i))] * DEPTH,
        out_shape=[jax.ShapeDtypeStruct((each, width), jnp.bfloat16)] * sent
        + [pltpu.HBM((each, width), jnp.float32)] * (DEPTH - sent),
        compiler_params=params(24),
        cost_estimate=pl.CostEstimate(flops=0, bytes_accessed=0, transcendentals=0),
        name="combine",
    )(rows, *in_hbm(tables))


def front_kernel(rows_ref, gate_ref, up_ref, down_ref, out_ref, total):
    step = pl.program_id(0)
    rows = rows_ref[...]
    gate = dot(rows, gate_ref[...])
    upper = dot(rows, up_ref[...])
    hidden = (gate * jax.nn.sigmoid(gate) * upper).astype(jnp.bfloat16)
    produced = dot(hidden, down_ref[...])

    @pl.when(step == 0)
    def _():
        total[...] = produced

    @pl.when(step > 0)
    def _():
        total[...] += produced

    @pl.when(step == pl.num_programs(0) - 1)
    def _():
        out_ref[...] = total[...].astype(jnp.bfloat16)


def back_kernel(rows_ref, grads_ref, gate_ref, up_ref, down_ref, out_ref, total):
    step = pl.program_id(0)
    rows = rows_ref[...]
    gate = dot(rows, gate_ref[...])
    upper = dot(rows, up_ref[...])
    sigma = jax.nn.sigmoid(gate)
    hidden_grad = dot_t(grads_ref[...], down_ref[...])
    gate_grad = (hidden_grad * upper * sigma * (1.0 + gate * (1.0 - sigma))).astype(jnp.bfloat16)
    upper_grad = (hidden_grad * gate * sigma).astype(jnp.bfloat16)
    produced = dot_t(gate_grad, gate_ref[...]) + dot_t(upper_grad, up_ref[...])

    @pl.when(step == 0)
    def _():
        total[...] = produced

    @pl.when(step > 0)
    def _():
        total[...] += produced

    @pl.when(step == pl.num_programs(0) - 1)
    def _():
        out_ref[...] = total[...].astype(jnp.bfloat16)


def expert(kernel, inputs, gate_matrix, up_matrix, down_matrix, products, name):
    width, units = gate_matrix.shape
    slots = inputs[0].shape[0]
    cut = 256
    tall = pl.BlockSpec((width, cut), lambda i: (0, i))
    flat = pl.BlockSpec((cut, width), lambda i: (i, 0))
    return pl.pallas_call(
        kernel,
        grid=(units // cut,),
        in_specs=[whole_spec(inputs[0].shape)] * len(inputs) + [tall, tall, flat],
        out_specs=whole_spec(inputs[0].shape),
        out_shape=pltpu.HBM(inputs[0].shape, jnp.bfloat16),
        scratch_shapes=[pltpu.VMEM((slots, width), jnp.float32)],
        compiler_params=params(40),
        cost_estimate=pl.CostEstimate(
            flops=2 * products * slots * width * units,
            bytes_accessed=16 * MIB,
            transcendentals=slots * units,
        ),
        name=name,
    )(*inputs, *in_hbm((gate_matrix, up_matrix, down_matrix)))


def exchange(rows):
    split = rows.reshape(EXPERTS, EACH, rows.shape[1])
    split = lax.all_to_all(split, ("y", "x"), split_axis=0, concat_axis=0, tiled=True)
    return split.reshape(rows.shape)


def local(
    front_tokens,
    front_experts,
    front_probs,
    back_tokens,
    back_experts,
    back_probs,
    back_grads,
    gate_weight,
    up_weight,
    down_weight,
):
    weights = (gate_weight[0, 0], up_weight[0, 0], down_weight[0, 0])
    width = back_tokens.shape[2]
    packed = pack(front_experts[0], front_probs[0], back_experts[0], back_probs[0], back_tokens[0])
    first, grads_all = gathered_pair(packed, back_grads[0])
    placed, column, share = first_place(first, width)
    back_rows = exchange(placed)
    front_all = gathered(front_tokens[0], (placed,), (back_rows,))
    placed = place(grads_all, column, share, 1, True, width)
    grad_rows = exchange(after(placed, front_all[1], front_all[8]))
    placed = place(front_all, column, share, 0, False, width)
    front_rows = exchange(placed)

    grad_rows = after(grad_rows, placed)
    produced = expert(back_kernel, (back_rows, grad_rows), *weights, 5, "back")
    back_home = exchange(after(produced, front_rows))
    back_table, *front_tables = weigh(column, share)
    front_rows = after(front_rows, back_table)
    produced = expert(front_kernel, (front_rows,), *weights, 3, "front")
    back_home = after(back_home, produced)
    front_home = exchange(produced)

    sums = combine(back_home, [back_table])
    front_home = after(front_home, *returned(sums, -1)[1])
    layer_out, came = returned(combine(front_home, front_tables), 1)
    input_grad, _ = returned(sums, -1, came)
    return layer_out[None], input_grad[None]


def solution(mesh):
    fine = Mesh(mesh.devices.reshape(4, DEPTH, WIDE, LONG), ("section", "z", "y", "x"))
    split = ("z", "y", "x")
    data = P("section", split, None)
    weight = P("section", split, None, None)
    return jax.shard_map(
        local,
        mesh=fine,
        in_specs=(data,) * 7 + (weight,) * 3,
        out_specs=(data, data),
        check_vma=False,
    )
```

```python
import functools

import jax
import jax.numpy as jnp
from jax import lax
from jax.experimental import pallas as pl
from jax.experimental.pallas import tpu as pltpu
from jax.sharding import Mesh, PartitionSpec as P

MOST = 9
DEPTH, WIDE, LONG = 8, 2, 4
EXPERTS = WIDE * LONG
EACH = DEPTH * MOST
SLOTS = EXPERTS * EACH
ORDER = (0, 4, 3, 5, 2, 6, 1, 7)
LANES = 128
MIB = 1024 * 1024


def along(block, distance, hop=0):
    n = lax.axis_size("section")
    route = []
    for s in range(n):
        for z in range(DEPTH):
            route.append((s * DEPTH + z, (s + hop) % n * DEPTH + (z + distance) % DEPTH))
    return lax.ppermute(block, ("section", "z"), route)


def after(block, *others):
    return lax.optimization_barrier((block,) + others)[0]


def ends(up, down):
    half = up.shape[0] // 2
    return [along(up[:half], 1), along(down[half:], -1)]


def gathered(block, early, late):
    block = after(block, *early)
    up1, down1 = along(block, 1), along(block, -1)
    up1, down1 = after(up1, *late), after(down1, *late)
    up2, down2 = along(up1, 1), along(down1, -1)
    up3, down3 = along(up2, 1), along(down2, -1)
    return [block, up1, up2, up3] + ends(up3, down3) + [down3, down2, down1]


def gathered_pair(a, b):
    ups, downs = [a], [a]
    others_up, others_down = [b], [b]
    for step in range(1, DEPTH // 2):
        up, down = ups[-1], downs[-1]
        if step == 3:
            other = (others_up[2], others_down[2])
            up, down = after(up, *other), after(down, *other)
        ups.append(along(up, 1))
        downs.append(along(down, -1))
        others_up.append(along(others_up[-1], 1))
        others_down.append(along(others_down[-1], -1))
    first = ups + ends(ups[3], downs[3]) + downs[:0:-1]
    second = others_up + ends(others_up[3], others_down[3]) + others_down[:0:-1]
    return first, second


def summed(parts):
    own, middle, low3, high3, low2, high2, low1, high1 = parts
    half = middle.shape[0] // 2
    down, up = along(middle[:half], -1), along(middle[half:], 1)
    down = jnp.pad(down.astype(jnp.float32), ((0, half), (0, 0)))
    up = jnp.pad(up.astype(jnp.float32), ((half, 0), (0, 0)))
    low3 = (low3 + down).astype(jnp.bfloat16)
    high3 = (high3 + up).astype(jnp.bfloat16)
    down, up = along(low3, -1), along(high3, 1)
    came = (down, up)
    low2 = (low2 + down.astype(jnp.float32)).astype(jnp.bfloat16)
    high2 = (high2 + up.astype(jnp.float32)).astype(jnp.bfloat16)
    down, up = along(low2, -1), along(high2, 1)
    low1 = (low1 + down.astype(jnp.float32)).astype(jnp.bfloat16)
    high1 = (high1 + up.astype(jnp.float32)).astype(jnp.bfloat16)
    return own, low1, high1, came


def returned(parts, hop):
    own, low1, high1, came = parts
    down, up = along(low1, -1, hop), along(high1, 1, hop)
    total = sum(one.astype(jnp.float32) for one in (along(own, 0, hop), down, up))
    return total.astype(jnp.bfloat16)


def finished(parts):
    own, low1, high1, _ = parts
    down, up = along(low1, -1), along(high1, 1)
    return sum(one.astype(jnp.float32) for one in (own, down, up)).astype(jnp.bfloat16)


def dot(a, b):
    return jnp.dot(a, b, preferred_element_type=jnp.float32)


def dot_t(a, b):
    return lax.dot_general(a, b, (((1,), (1,)), ((), ())), preferred_element_type=jnp.float32)


def split3(value):
    high = value.astype(jnp.bfloat16)
    value = value - high.astype(jnp.float32)
    middle = value.astype(jnp.bfloat16)
    value = value - middle.astype(jnp.float32)
    return high, middle, value.astype(jnp.bfloat16)


def bits(mask):
    return jnp.where(mask, 1.0, 0.0).astype(jnp.bfloat16)


def make_plan(meta, plane):
    square = (LANES, LANES)
    i = lax.broadcasted_iota(jnp.int32, square, 0)
    c = lax.broadcasted_iota(jnp.int32, square, 1)
    side, pick, kind = c >> 6, (c >> 3) & 7, c & 7
    probs = (i >= 16 + side * 24) & (i < 40 + side * 24)
    chosen = dot(meta, bits(i == side * 8 + pick))
    prob = dot(meta, bits(probs & ((i & 7) == pick)))
    whole = dot(meta, bits(probs))
    shape = chosen.shape
    lane = lax.broadcasted_iota(jnp.int32, shape, 1)
    label = (plane * EXPERTS + (lane & 7)).astype(jnp.float32)
    hit = chosen == label
    pairs = bits((c < 16) & ((i & 7) == (c & 7)) & ((i >> 6) == (c >> 3)))
    named = dot(bits(hit), pairs)
    share = jnp.where(hit, prob / whole, 0.0)
    share = sum(dot(part, pairs) for part in split3(share))
    rows = shape[0]
    a = lax.broadcasted_iota(jnp.int32, (rows, rows), 0)
    b = lax.broadcasted_iota(jnp.int32, (rows, rows), 1)
    earlier = bits((b < a) & ((a >> 6) == (b >> 6)))
    rank = dot(earlier, named.astype(jnp.bfloat16)).astype(jnp.int32)
    row = lax.broadcasted_iota(jnp.int32, shape, 0)
    column = (lane & 7) * EACH + (row >> 6) * MOST + rank
    return jnp.where(named > 0.5, column, -1), share


def spread_tiles(column, share, side):
    tiles = []
    for start in range(0, SLOTS, LANES):
        stop = min(start + LANES, SLOTS)
        shape = (column.shape[0], stop - start)
        slot = lax.broadcasted_iota(jnp.int32, shape, 1) + start
        total = jnp.zeros(shape, jnp.float32)
        for j in range(start // EACH, -(-stop // EACH)):
            lane = side * EXPERTS + j
            value = 1.0 if share is None else share[:, lane : lane + 1]
            total = jnp.where(slot == column[:, lane : lane + 1], value, total)
        tiles.append((start, stop, total))
    return tiles


def fill(tables, column, share, side, turned):
    for start, stop, tile in spread_tiles(column, share, side):
        if turned:
            tile = tile.T
        for table in tables:
            part = tile.astype(jnp.bfloat16)
            tile = tile - part.astype(jnp.float32)
            if turned:
                table[start:stop, :] = part
            else:
                table[:, start:stop] = part


def first_kernel(*refs):
    n = DEPTH + 1
    plane_ref, pieces, metas = refs[0], refs[1 : 1 + n], refs[1 + n : 1 + 2 * n]
    rows_ref, column_ref, share_ref, table, stack = refs[1 + 2 * n :]

    @pl.when(pl.program_id(0) == 0)
    def _():
        meta = jnp.concatenate([ref[...] for ref in metas], axis=0)
        column, share = make_plan(meta, plane_ref[0])
        column_ref[...] = column
        share_ref[...] = share
        fill([table], column, None, 1, True)

    at = 0
    for ref in pieces:
        stack[at : at + ref.shape[0], :] = ref[...]
        at += ref.shape[0]
    rows_ref[...] = dot(table[...], stack[...]).astype(jnp.bfloat16)


def place_kernel(side, weighted, n, *refs):
    pieces, column_ref, share_ref = refs[:n], refs[n], refs[n + 1]
    rows_ref, table, factor, stack = refs[n + 2 :]

    @pl.when(pl.program_id(0) == 0)
    def _():
        if weighted:
            for start, stop, tile in spread_tiles(column_ref[...], share_ref[...], side):
                tile = tile.T
                table[start:stop, :] = bits(tile > 0.0)
                factor[start:stop, :] = jnp.sum(tile, axis=1, keepdims=True)
        else:
            fill([table], column_ref[...], None, side, True)

    at = 0
    for ref in pieces:
        stack[at : at + ref.shape[0], :] = ref[...]
        at += ref.shape[0]
    rows = dot(table[...], stack[...])
    if weighted:
        rows = rows * factor[...]
    rows_ref[...] = rows.astype(jnp.bfloat16)


def weigh_kernel(sides, column_ref, share_ref, *tables):
    for side, weighted in sides:
        share = share_ref[...] if weighted else None
        fill(tables[:1], column_ref[...], share, side, False)
        tables = tables[1:]


def combine_kernel(count, rows_ref, *refs):
    tables, outs = refs[:count], refs[count:]
    rows = rows_ref[...]
    total = sum(dot(table[...], rows) for table in tables)
    tokens = total.shape[0] // DEPTH
    for k, ref in zip(ORDER, outs):
        ref[...] = total[k * tokens : (k + 1) * tokens].astype(ref.dtype)


def pack_kernel(fe_ref, fp_ref, be_ref, bp_ref, rows_ref, out_ref):
    width = rows_ref.shape[1]
    out_ref[:, :width] = rows_ref[...]
    parts = [fe_ref[...].astype(jnp.float32), be_ref[...].astype(jnp.float32)]
    for ref in (fp_ref, bp_ref):
        parts += [part.astype(jnp.float32) for part in split3(ref[...])]
    used = sum(part.shape[0] for part in parts)
    parts.append(jnp.zeros((LANES - used, parts[0].shape[1]), jnp.float32))
    out_ref[:, width:] = jnp.concatenate(parts, axis=0).T.astype(jnp.bfloat16)


def pack(front_experts, front_probs, back_experts, back_probs, rows):
    tokens, width = rows.shape
    inputs = (front_experts.T, front_probs.T, back_experts.T, back_probs.T, rows)
    return pl.pallas_call(
        pack_kernel,
        out_shape=jax.ShapeDtypeStruct((tokens, width + LANES), jnp.bfloat16),
        compiler_params=pltpu.CompilerParams(vmem_limit_bytes=24 * MIB),
        name="pack",
    )(*in_hbm(inputs))


STEPS, FINE = 2, 2


def in_hbm(arrays):
    return [pltpu.with_memory_space_constraint(array, pltpu.HBM) for array in arrays]


def params(limit):
    return pltpu.CompilerParams(vmem_limit_bytes=limit * MIB, dimension_semantics=("arbitrary",))


def piece_specs(pieces, width, start=0):
    at = start // (width // STEPS)
    return [pl.BlockSpec((p.shape[0], width // STEPS), lambda i: (0, i + at)) for p in pieces]


def whole_spec(shape):
    return pl.BlockSpec(shape, lambda i: (0, 0))


def first_place(pieces, width):
    tokens = sum(p.shape[0] for p in pieces)
    slots = EXPERTS * EACH
    last = pieces[0].shape[1] // LANES - 1
    metas = [pl.BlockSpec((p.shape[0], LANES), lambda i: (0, last)) for p in pieces]
    plan = (tokens, LANES)
    return pl.pallas_call(
        first_kernel,
        grid=(STEPS,),
        in_specs=[pl.BlockSpec(memory_space=pltpu.SMEM)] + piece_specs(pieces, width) + metas,
        out_specs=[
            pl.BlockSpec((slots, width // STEPS), lambda i: (0, i)),
            whole_spec(plan),
            whole_spec(plan),
        ],
        out_shape=[
            pltpu.HBM((slots, width), jnp.bfloat16),
            pltpu.HBM(plan, jnp.int32),
            pltpu.HBM(plan, jnp.float32),
        ],
        scratch_shapes=[
            pltpu.VMEM((slots, tokens), jnp.bfloat16),
            pltpu.VMEM((tokens, width // STEPS), jnp.bfloat16),
        ],
        compiler_params=params(24),
        cost_estimate=pl.CostEstimate(
            flops=2 * slots * tokens * width, bytes_accessed=6 * MIB, transcendentals=0
        ),
        name="first_place",
    )(lax.axis_index("z").astype(jnp.int32).reshape(1), *in_hbm(pieces), *in_hbm(pieces))


def place(pieces, column, share, side, weighted, width, start=0):
    tokens = sum(p.shape[0] for p in pieces)
    slots = EXPERTS * EACH
    return pl.pallas_call(
        functools.partial(place_kernel, side, weighted, len(pieces)),
        grid=(STEPS,),
        in_specs=piece_specs(pieces, width, start) + [whole_spec(column.shape)] * 2,
        out_specs=pl.BlockSpec((slots, width // STEPS), lambda i: (0, i)),
        out_shape=pltpu.HBM((slots, width), jnp.bfloat16),
        scratch_shapes=[
            pltpu.VMEM((slots, tokens), jnp.bfloat16),
            pltpu.VMEM((slots, 1), jnp.float32),
            pltpu.VMEM((tokens, width // STEPS), jnp.bfloat16),
        ],
        compiler_params=params(24),
        cost_estimate=pl.CostEstimate(
            flops=2 * slots * tokens * width, bytes_accessed=6 * MIB, transcendentals=0
        ),
        name="place",
    )(*in_hbm(pieces + [column, share]))


def weigh(column, share):
    sides = (1, False), (0, True)
    table = jax.ShapeDtypeStruct((column.shape[0], SLOTS), jnp.bfloat16)
    return pl.pallas_call(
        functools.partial(weigh_kernel, sides),
        out_shape=[pltpu.HBM(table.shape, table.dtype)] * 2,
        compiler_params=pltpu.CompilerParams(vmem_limit_bytes=24 * MIB),
        cost_estimate=pl.CostEstimate(flops=0, bytes_accessed=2 * MIB, transcendentals=0),
        name="weigh",
    )(*in_hbm((column, share)))


def combine(rows, tables, kept):
    slots, width = rows.shape
    tokens = tables[0].shape[0]
    each = tokens // DEPTH
    sent = 2
    return pl.pallas_call(
        functools.partial(combine_kernel, len(tables)),
        grid=(FINE,),
        in_specs=[pl.BlockSpec((slots, width // FINE), lambda i: (0, i))]
        + [whole_spec(table.shape) for table in tables],
        out_specs=[pl.BlockSpec((each, width // FINE), lambda i: (0, i))] * DEPTH,
        out_shape=[jax.ShapeDtypeStruct((each, width), jnp.bfloat16)] * sent
        + [kept((each, width), jnp.float32)] * (DEPTH - sent),
        compiler_params=params(24),
        cost_estimate=pl.CostEstimate(flops=0, bytes_accessed=0, transcendentals=0),
        name="combine",
    )(rows, *in_hbm(tables))


def front_kernel(rows_ref, gate_ref, up_ref, down_ref, out_ref, total):
    step = pl.program_id(0)
    rows = rows_ref[...]
    gate = dot(rows, gate_ref[...])
    upper = dot(rows, up_ref[...])
    hidden = (gate * jax.nn.sigmoid(gate) * upper).astype(jnp.bfloat16)
    produced = dot(hidden, down_ref[...])

    @pl.when(step == 0)
    def _():
        total[...] = produced

    @pl.when(step > 0)
    def _():
        total[...] += produced

    @pl.when(step == pl.num_programs(0) - 1)
    def _():
        out_ref[...] = total[...].astype(jnp.bfloat16)


def back_kernel(rows_ref, grads_ref, gate_ref, up_ref, down_ref, out_ref, total):
    step = pl.program_id(0)
    rows = rows_ref[...]
    gate = dot(rows, gate_ref[...])
    upper = dot(rows, up_ref[...])
    sigma = jax.nn.sigmoid(gate)
    hidden_grad = dot_t(grads_ref[...], down_ref[...])
    gate_grad = (hidden_grad * upper * sigma * (1.0 + gate * (1.0 - sigma))).astype(jnp.bfloat16)
    upper_grad = (hidden_grad * gate * sigma).astype(jnp.bfloat16)
    produced = dot_t(gate_grad, gate_ref[...]) + dot_t(upper_grad, up_ref[...])

    @pl.when(step == 0)
    def _():
        total[...] = produced

    @pl.when(step > 0)
    def _():
        total[...] += produced

    @pl.when(step == pl.num_programs(0) - 1)
    def _():
        out_ref[...] = total[...].astype(jnp.bfloat16)


def expert(kernel, inputs, gate_matrix, up_matrix, down_matrix, products, name):
    width, units = gate_matrix.shape
    slots = inputs[0].shape[0]
    cut = 256
    tall = pl.BlockSpec((width, cut), lambda i: (0, i))
    flat = pl.BlockSpec((cut, width), lambda i: (i, 0))
    return pl.pallas_call(
        kernel,
        grid=(units // cut,),
        in_specs=[whole_spec(inputs[0].shape)] * len(inputs) + [tall, tall, flat],
        out_specs=whole_spec(inputs[0].shape),
        out_shape=pltpu.HBM(inputs[0].shape, jnp.bfloat16),
        scratch_shapes=[pltpu.VMEM((slots, width), jnp.float32)],
        compiler_params=params(40),
        cost_estimate=pl.CostEstimate(
            flops=2 * products * slots * width * units,
            bytes_accessed=16 * MIB,
            transcendentals=slots * units,
        ),
        name=name,
    )(*inputs, *in_hbm((gate_matrix, up_matrix, down_matrix)))


def exchange(rows):
    split = rows.reshape(EXPERTS, EACH, rows.shape[1])
    split = lax.all_to_all(split, ("y", "x"), split_axis=0, concat_axis=0, tiled=True)
    return split.reshape(rows.shape)


def local(
    front_tokens,
    front_experts,
    front_probs,
    back_tokens,
    back_experts,
    back_probs,
    back_grads,
    gate_weight,
    up_weight,
    down_weight,
):
    weights = (gate_weight[0, 0], up_weight[0, 0], down_weight[0, 0])
    width = back_tokens.shape[2]
    packed = pack(front_experts[0], front_probs[0], back_experts[0], back_probs[0], back_tokens[0])
    first, grads_all = gathered_pair(packed, back_grads[0])
    placed, column, share = first_place(first, width)
    back_rows = exchange(placed)
    front_all = gathered(front_tokens[0], (placed,), (back_rows,))
    placed = place(grads_all, column, share, 1, True, width)
    grad_rows = exchange(after(placed, front_all[1], front_all[8]))
    placed = place(front_all, column, share, 0, False, width)
    front_rows = exchange(placed)

    grad_rows = after(grad_rows, placed)
    produced = expert(back_kernel, (back_rows, grad_rows), *weights, 5, "back")
    back_home = exchange(after(produced, front_rows))
    back_table, *front_tables = weigh(column, share)
    front_rows = after(front_rows, back_table)
    produced = expert(front_kernel, (front_rows,), *weights, 3, "front")
    back_home = after(back_home, produced)
    front_home = exchange(produced)

    total = finished(summed(combine(back_home, [back_table], pltpu.HBM)))
    front_home = after(front_home, total)
    front_sums = summed(combine(front_home, front_tables, pltpu.VMEM))
    own, low1, high1, third = front_sums
    input_grad = along(after(total, *third), 0, -1)
    layer_out = returned((own, after(low1, input_grad), after(high1, input_grad), third), 1)
    return layer_out[None], input_grad[None]


def solution(mesh):
    fine = Mesh(mesh.devices.reshape(4, DEPTH, WIDE, LONG), ("section", "z", "y", "x"))
    split = ("z", "y", "x")
    data = P("section", split, None)
    weight = P("section", split, None, None)
    return jax.shard_map(
        local,
        mesh=fine,
        in_specs=(data,) * 7 + (weight,) * 3,
        out_specs=(data, data),
        check_vma=False,
    )
```

```python
import functools

import jax
import jax.numpy as jnp
from jax import lax
from jax.experimental import pallas as pl
from jax.experimental.pallas import tpu as pltpu
from jax.sharding import Mesh, PartitionSpec as P

MOST = 9
DEPTH, WIDE, LONG = 8, 2, 4
EXPERTS = WIDE * LONG
EACH = DEPTH * MOST
SLOTS = EXPERTS * EACH
ORDER = (0, 4, 3, 5, 2, 6, 1, 7)
LANES = 128
MIB = 1024 * 1024


def along(block, distance, hop=0):
    n = lax.axis_size("section")
    route = []
    for s in range(n):
        for z in range(DEPTH):
            route.append((s * DEPTH + z, (s + hop) % n * DEPTH + (z + distance) % DEPTH))
    return lax.ppermute(block, ("section", "z"), route)


def after(block, *others):
    return lax.optimization_barrier((block,) + others)[0]


def ends(up, down):
    half = up.shape[0] // 2
    return [along(up[:half], 1), along(down[half:], -1)]


def gathered(block, early, late):
    block = after(block, *early)
    up1, down1 = along(block, 1), along(block, -1)
    up1, down1 = after(up1, *late), after(down1, *late)
    up2, down2 = along(up1, 1), along(down1, -1)
    up3, down3 = along(up2, 1), along(down2, -1)
    return [block, up1, up2, up3, along(up3, 1), down3, down2, down1]


def gathered_pair(a, b):
    ups, downs = [a], [a]
    others_up, others_down = [b], [b]
    for step in range(1, DEPTH // 2):
        up, down = ups[-1], downs[-1]
        if step == 3:
            other = (others_up[2], others_down[2])
            up, down = after(up, *other), after(down, *other)
        ups.append(along(up, 1))
        downs.append(along(down, -1))
        others_up.append(along(others_up[-1], 1))
        others_down.append(along(others_down[-1], -1))
    first = ups + ends(ups[3], downs[3]) + downs[:0:-1]
    second = others_up + [along(others_up[3], 1)] + others_down[:0:-1]
    return first, second


def summed(parts):
    own, middle, low3, high3, low2, high2, low1, high1 = parts
    half = middle.shape[0] // 2
    down, up = along(middle[:half], -1), along(middle[half:], 1)
    down = jnp.pad(down.astype(jnp.float32), ((0, half), (0, 0)))
    up = jnp.pad(up.astype(jnp.float32), ((half, 0), (0, 0)))
    low3 = (low3 + down).astype(jnp.bfloat16)
    high3 = (high3 + up).astype(jnp.bfloat16)
    down, up = along(low3, -1), along(high3, 1)
    came = (down, up)
    low2 = (low2 + down.astype(jnp.float32)).astype(jnp.bfloat16)
    high2 = (high2 + up.astype(jnp.float32)).astype(jnp.bfloat16)
    down, up = along(low2, -1), along(high2, 1)
    low1 = (low1 + down.astype(jnp.float32)).astype(jnp.bfloat16)
    high1 = (high1 + up.astype(jnp.float32)).astype(jnp.bfloat16)
    return own, low1, high1, came


def returned(parts, hop):
    own, low1, high1, came = parts
    down, up = along(low1, -1, hop), along(high1, 1, hop)
    total = sum(one.astype(jnp.float32) for one in (along(own, 0, hop), down, up))
    return total.astype(jnp.bfloat16)


def finished(parts):
    own, low1, high1, _ = parts
    down, up = along(low1, -1), along(high1, 1)
    return sum(one.astype(jnp.float32) for one in (own, down, up)).astype(jnp.bfloat16)


def dot(a, b):
    return jnp.dot(a, b, preferred_element_type=jnp.float32)


def dot_t(a, b):
    return lax.dot_general(a, b, (((1,), (1,)), ((), ())), preferred_element_type=jnp.float32)


def split3(value):
    high = value.astype(jnp.bfloat16)
    value = value - high.astype(jnp.float32)
    middle = value.astype(jnp.bfloat16)
    value = value - middle.astype(jnp.float32)
    return high, middle, value.astype(jnp.bfloat16)


def bits(mask):
    return jnp.where(mask, 1.0, 0.0).astype(jnp.bfloat16)


def make_plan(meta, plane):
    square = (LANES, LANES)
    i = lax.broadcasted_iota(jnp.int32, square, 0)
    c = lax.broadcasted_iota(jnp.int32, square, 1)
    side, pick, kind = c >> 6, (c >> 3) & 7, c & 7
    probs = (i >= 16 + side * 24) & (i < 40 + side * 24)
    chosen = dot(meta, bits(i == side * 8 + pick))
    prob = dot(meta, bits(probs & ((i & 7) == pick)))
    whole = dot(meta, bits(probs))
    shape = chosen.shape
    lane = lax.broadcasted_iota(jnp.int32, shape, 1)
    label = (plane * EXPERTS + (lane & 7)).astype(jnp.float32)
    hit = chosen == label
    pairs = bits((c < 16) & ((i & 7) == (c & 7)) & ((i >> 6) == (c >> 3)))
    named = dot(bits(hit), pairs)
    share = jnp.where(hit, prob / whole, 0.0)
    share = sum(dot(part, pairs) for part in split3(share))
    rows = shape[0]
    a = lax.broadcasted_iota(jnp.int32, (rows, rows), 0)
    b = lax.broadcasted_iota(jnp.int32, (rows, rows), 1)
    earlier = bits((b < a) & ((a >> 6) == (b >> 6)))
    rank = dot(earlier, named.astype(jnp.bfloat16)).astype(jnp.int32)
    row = lax.broadcasted_iota(jnp.int32, shape, 0)
    column = (lane & 7) * EACH + (row >> 6) * MOST + rank
    return jnp.where(named > 0.5, column, -1), share


def spread_tiles(column, share, side):
    tiles = []
    for start in range(0, SLOTS, LANES):
        stop = min(start + LANES, SLOTS)
        shape = (column.shape[0], stop - start)
        slot = lax.broadcasted_iota(jnp.int32, shape, 1) + start
        total = jnp.zeros(shape, jnp.float32)
        for j in range(start // EACH, -(-stop // EACH)):
            lane = side * EXPERTS + j
            value = 1.0 if share is None else share[:, lane : lane + 1]
            total = jnp.where(slot == column[:, lane : lane + 1], value, total)
        tiles.append((start, stop, total))
    return tiles


def fill(tables, column, share, side, turned):
    for start, stop, tile in spread_tiles(column, share, side):
        if turned:
            tile = tile.T
        for table in tables:
            part = tile.astype(jnp.bfloat16)
            tile = tile - part.astype(jnp.float32)
            if turned:
                table[start:stop, :] = part
            else:
                table[:, start:stop] = part


def first_kernel(*refs):
    n = DEPTH + 1
    plane_ref, pieces, metas = refs[0], refs[1 : 1 + n], refs[1 + n : 1 + 2 * n]
    rows_ref, column_ref, share_ref, table, stack = refs[1 + 2 * n :]

    @pl.when(pl.program_id(0) == 0)
    def _():
        meta = jnp.concatenate([ref[...] for ref in metas], axis=0)
        column, share = make_plan(meta, plane_ref[0])
        column_ref[...] = column
        share_ref[...] = share
        fill([table], column, None, 1, True)

    at = 0
    for ref in pieces:
        stack[at : at + ref.shape[0], :] = ref[...]
        at += ref.shape[0]
    rows_ref[...] = dot(table[...], stack[...]).astype(jnp.bfloat16)


def weighted_kernel(n, *refs):
    pieces, column_ref, share_ref = refs[:n], refs[n], refs[n + 1]
    rows_ref, other_ref, table, factor, stack = refs[n + 2 :]

    @pl.when(pl.program_id(0) == 0)
    def _():
        for start, stop, tile in spread_tiles(column_ref[...], share_ref[...], 1):
            tile = tile.T
            table[start:stop, :] = bits(tile > 0.0)
            factor[start:stop, :] = jnp.sum(tile, axis=1, keepdims=True)
        fill([other_ref], column_ref[...], None, 0, True)

    at = 0
    for ref in pieces:
        stack[at : at + ref.shape[0], :] = ref[...]
        at += ref.shape[0]
    rows_ref[...] = (dot(table[...], stack[...]) * factor[...]).astype(jnp.bfloat16)


def place_kernel(n, *refs):
    pieces, table_ref, rows_ref, stack = refs[:n], refs[n], refs[n + 1], refs[n + 2]
    at = 0
    for ref in pieces:
        stack[at : at + ref.shape[0], :] = ref[...]
        at += ref.shape[0]
    rows_ref[...] = dot(table_ref[...], stack[...]).astype(jnp.bfloat16)


def weigh_kernel(sides, column_ref, share_ref, *tables):
    for side, weighted in sides:
        share = share_ref[...] if weighted else None
        fill(tables[:1], column_ref[...], share, side, False)
        tables = tables[1:]


def combine_kernel(count, rows_ref, *refs):
    tables, outs = refs[:count], refs[count:]
    rows = rows_ref[...]
    total = sum(dot(table[...], rows) for table in tables)
    tokens = total.shape[0] // DEPTH
    for k, ref in zip(ORDER, outs):
        ref[...] = total[k * tokens : (k + 1) * tokens].astype(ref.dtype)


def pack_kernel(fe_ref, fp_ref, be_ref, bp_ref, rows_ref, out_ref):
    width = rows_ref.shape[1]
    out_ref[:, :width] = rows_ref[...]
    parts = [fe_ref[...].astype(jnp.float32), be_ref[...].astype(jnp.float32)]
    for ref in (fp_ref, bp_ref):
        parts += [part.astype(jnp.float32) for part in split3(ref[...])]
    used = sum(part.shape[0] for part in parts)
    parts.append(jnp.zeros((LANES - used, parts[0].shape[1]), jnp.float32))
    out_ref[:, width:] = jnp.concatenate(parts, axis=0).T.astype(jnp.bfloat16)


def pack(front_experts, front_probs, back_experts, back_probs, rows):
    tokens, width = rows.shape
    inputs = (front_experts.T, front_probs.T, back_experts.T, back_probs.T, rows)
    return pl.pallas_call(
        pack_kernel,
        out_shape=jax.ShapeDtypeStruct((tokens, width + LANES), jnp.bfloat16),
        compiler_params=pltpu.CompilerParams(vmem_limit_bytes=24 * MIB),
        name="pack",
    )(*in_hbm(inputs))


STEPS, FINE = 2, 2


def in_hbm(arrays):
    return [pltpu.with_memory_space_constraint(array, pltpu.HBM) for array in arrays]


def params(limit):
    return pltpu.CompilerParams(vmem_limit_bytes=limit * MIB, dimension_semantics=("arbitrary",))


def piece_specs(pieces, width, start=0):
    at = start // (width // STEPS)
    return [pl.BlockSpec((p.shape[0], width // STEPS), lambda i: (0, i + at)) for p in pieces]


def whole_spec(shape):
    return pl.BlockSpec(shape, lambda i: (0, 0))


def first_place(pieces, width):
    tokens = sum(p.shape[0] for p in pieces)
    slots = EXPERTS * EACH
    last = pieces[0].shape[1] // LANES - 1
    metas = [pl.BlockSpec((p.shape[0], LANES), lambda i: (0, last)) for p in pieces]
    plan = (tokens, LANES)
    return pl.pallas_call(
        first_kernel,
        grid=(STEPS,),
        in_specs=[pl.BlockSpec(memory_space=pltpu.SMEM)] + piece_specs(pieces, width) + metas,
        out_specs=[
            pl.BlockSpec((slots, width // STEPS), lambda i: (0, i)),
            whole_spec(plan),
            whole_spec(plan),
        ],
        out_shape=[
            pltpu.HBM((slots, width), jnp.bfloat16),
            pltpu.HBM(plan, jnp.int32),
            pltpu.HBM(plan, jnp.float32),
        ],
        scratch_shapes=[
            pltpu.VMEM((slots, tokens), jnp.bfloat16),
            pltpu.VMEM((tokens, width // STEPS), jnp.bfloat16),
        ],
        compiler_params=params(24),
        cost_estimate=pl.CostEstimate(
            flops=2 * slots * tokens * width, bytes_accessed=6 * MIB, transcendentals=0
        ),
        name="first_place",
    )(lax.axis_index("z").astype(jnp.int32).reshape(1), *in_hbm(pieces), *in_hbm(pieces))


def place_weighted(pieces, column, share, width):
    tokens = sum(p.shape[0] for p in pieces)
    table = (SLOTS, tokens)
    return pl.pallas_call(
        functools.partial(weighted_kernel, len(pieces)),
        grid=(STEPS,),
        in_specs=piece_specs(pieces, width) + [whole_spec(column.shape)] * 2,
        out_specs=[pl.BlockSpec((SLOTS, width // STEPS), lambda i: (0, i)), whole_spec(table)],
        out_shape=[pltpu.HBM((SLOTS, width), jnp.bfloat16), pltpu.HBM(table, jnp.bfloat16)],
        scratch_shapes=[
            pltpu.VMEM(table, jnp.bfloat16),
            pltpu.VMEM((SLOTS, 1), jnp.float32),
            pltpu.VMEM((tokens, width // STEPS), jnp.bfloat16),
        ],
        compiler_params=params(24),
        cost_estimate=pl.CostEstimate(
            flops=2 * SLOTS * tokens * width, bytes_accessed=6 * MIB, transcendentals=0
        ),
        name="place_weighted",
    )(*in_hbm(pieces + [column, share]))


def place(pieces, table, width):
    tokens = sum(p.shape[0] for p in pieces)
    return pl.pallas_call(
        functools.partial(place_kernel, len(pieces)),
        grid=(STEPS,),
        in_specs=piece_specs(pieces, width) + [whole_spec(table.shape)],
        out_specs=pl.BlockSpec((SLOTS, width // STEPS), lambda i: (0, i)),
        out_shape=pltpu.HBM((SLOTS, width), jnp.bfloat16),
        scratch_shapes=[pltpu.VMEM((tokens, width // STEPS), jnp.bfloat16)],
        compiler_params=params(24),
        cost_estimate=pl.CostEstimate(
            flops=2 * SLOTS * tokens * width, bytes_accessed=6 * MIB, transcendentals=0
        ),
        name="place",
    )(*in_hbm(pieces + [table]))


def weigh(column, share):
    sides = (1, False), (0, True)
    table = jax.ShapeDtypeStruct((column.shape[0], SLOTS), jnp.bfloat16)
    return pl.pallas_call(
        functools.partial(weigh_kernel, sides),
        out_shape=[pltpu.HBM(table.shape, table.dtype)] * 2,
        compiler_params=pltpu.CompilerParams(vmem_limit_bytes=24 * MIB),
        cost_estimate=pl.CostEstimate(flops=0, bytes_accessed=2 * MIB, transcendentals=0),
        name="weigh",
    )(*in_hbm((column, share)))


def combine(rows, tables, kept, sent):
    slots, width = rows.shape
    tokens = tables[0].shape[0]
    each = tokens // DEPTH
    return pl.pallas_call(
        functools.partial(combine_kernel, len(tables)),
        grid=(FINE,),
        in_specs=[pl.BlockSpec((slots, width // FINE), lambda i: (0, i))]
        + [whole_spec(table.shape) for table in tables],
        out_specs=[pl.BlockSpec((each, width // FINE), lambda i: (0, i))] * DEPTH,
        out_shape=[jax.ShapeDtypeStruct((each, width), jnp.bfloat16)] * sent
        + [kept((each, width), jnp.float32)] * (DEPTH - sent),
        compiler_params=params(24),
        cost_estimate=pl.CostEstimate(flops=0, bytes_accessed=0, transcendentals=0),
        name="combine",
    )(rows, *in_hbm(tables))


def front_kernel(rows_ref, gate_ref, up_ref, down_ref, out_ref, total):
    step = pl.program_id(0)
    rows = rows_ref[...]
    gate = dot(rows, gate_ref[...])
    upper = dot(rows, up_ref[...])
    hidden = (gate * jax.nn.sigmoid(gate) * upper).astype(jnp.bfloat16)
    produced = dot(hidden, down_ref[...])

    @pl.when(step == 0)
    def _():
        total[...] = produced

    @pl.when(step > 0)
    def _():
        total[...] += produced

    @pl.when(step == pl.num_programs(0) - 1)
    def _():
        out_ref[...] = total[...].astype(jnp.bfloat16)


def back_kernel(rows_ref, grads_ref, gate_ref, up_ref, down_ref, out_ref, total):
    step = pl.program_id(0)
    rows = rows_ref[...]
    gate = dot(rows, gate_ref[...])
    upper = dot(rows, up_ref[...])
    sigma = jax.nn.sigmoid(gate)
    hidden_grad = dot_t(grads_ref[...], down_ref[...])
    gate_grad = (hidden_grad * upper * sigma * (1.0 + gate * (1.0 - sigma))).astype(jnp.bfloat16)
    upper_grad = (hidden_grad * gate * sigma).astype(jnp.bfloat16)
    produced = dot_t(gate_grad, gate_ref[...]) + dot_t(upper_grad, up_ref[...])

    @pl.when(step == 0)
    def _():
        total[...] = produced

    @pl.when(step > 0)
    def _():
        total[...] += produced

    @pl.when(step == pl.num_programs(0) - 1)
    def _():
        out_ref[...] = total[...].astype(jnp.bfloat16)


def expert(kernel, inputs, gate_matrix, up_matrix, down_matrix, products, name):
    width, units = gate_matrix.shape
    slots = inputs[0].shape[0]
    cut = 256
    tall = pl.BlockSpec((width, cut), lambda i: (0, i))
    flat = pl.BlockSpec((cut, width), lambda i: (i, 0))
    return pl.pallas_call(
        kernel,
        grid=(units // cut,),
        in_specs=[whole_spec(inputs[0].shape)] * len(inputs) + [tall, tall, flat],
        out_specs=whole_spec(inputs[0].shape),
        out_shape=pltpu.HBM(inputs[0].shape, jnp.bfloat16),
        scratch_shapes=[pltpu.VMEM((slots, width), jnp.float32)],
        compiler_params=params(40),
        cost_estimate=pl.CostEstimate(
            flops=2 * products * slots * width * units,
            bytes_accessed=16 * MIB,
            transcendentals=slots * units,
        ),
        name=name,
    )(*inputs, *in_hbm((gate_matrix, up_matrix, down_matrix)))


def exchange(rows):
    split = rows.reshape(EXPERTS, EACH, rows.shape[1])
    split = lax.all_to_all(split, ("y", "x"), split_axis=0, concat_axis=0, tiled=True)
    return split.reshape(rows.shape)


def local(
    front_tokens,
    front_experts,
    front_probs,
    back_tokens,
    back_experts,
    back_probs,
    back_grads,
    gate_weight,
    up_weight,
    down_weight,
):
    weights = (gate_weight[0, 0], up_weight[0, 0], down_weight[0, 0])
    width = back_tokens.shape[2]
    packed = pack(front_experts[0], front_probs[0], back_experts[0], back_probs[0], back_tokens[0])
    first, grads_all = gathered_pair(packed, back_grads[0])
    placed, column, share = first_place(first, width)
    back_rows = exchange(placed)
    front_all = gathered(front_tokens[0], (placed,), (back_rows,))
    placed, table = place_weighted(grads_all, column, share, width)
    grad_rows = exchange(after(placed, front_all[1], front_all[7]))
    placed = place(front_all, table, width)
    front_rows = exchange(placed)

    grad_rows = after(grad_rows, placed)
    produced = expert(back_kernel, (back_rows, grad_rows), *weights, 5, "back")
    back_home = exchange(after(produced, front_rows))
    back_table, *front_tables = weigh(column, share)
    front_rows = after(front_rows, back_table)
    produced = expert(front_kernel, (front_rows,), *weights, 3, "front")
    back_home = after(back_home, produced)
    front_home = exchange(produced)

    total = finished(summed(combine(back_home, [back_table], pltpu.HBM, 2)))
    front_home = after(front_home, total)
    front_sums = summed(combine(front_home, front_tables, pltpu.VMEM, 2))
    own, low1, high1, third = front_sums
    input_grad = along(after(total, *third), 0, -1)
    layer_out = returned((own, after(low1, input_grad), after(high1, input_grad), third), 1)
    return layer_out[None], input_grad[None]


def solution(mesh):
    fine = Mesh(mesh.devices.reshape(4, DEPTH, WIDE, LONG), ("section", "z", "y", "x"))
    split = ("z", "y", "x")
    data = P("section", split, None)
    weight = P("section", split, None, None)
    return jax.shard_map(
        local,
        mesh=fine,
        in_specs=(data,) * 7 + (weight,) * 3,
        out_specs=(data, data),
        check_vma=False,
    )
```
